128 devices in a mesh: leaf: 4 (over y), row: 8 (over z, core), col: 4 (over x).
Axes of the slice: x: 4, y: 4, z: 4, core: 2. Of those that a mesh axis runs over, the one named last changes fastest.
Arguments:
- leaf_rhs: float32 [4, 8, 4, 1, 128, 256], P('leaf', 'row', 'col'), may hold values from -6 to 6
- mid_rhs: float32 [4, 8, 4, 1, 128, 256], P('leaf', 'row', 'col'), may hold values from -6 to 6
- top_rhs: float32 [4, 8, 4, 1, 128, 256], P('leaf', 'row', 'col'), may hold values from -6 to 6
- leaf_inverse: bfloat16 [4, 8, 4, 128, 4, 8, 128], P('leaf', 'row', None, None, 'col'), as said below
- mid_inverse: bfloat16 [4, 8, 4, 128, 4, 16, 128], P('leaf', 'row', None, None, 'col'), as said below
- top_inverse: bfloat16 [4, 8, 4, 128, 4, 32, 128], P('leaf', 'row', None, None, 'col'), as said below
- leaf_coupling: bfloat16 [4, 8, 4, 6, 128, 4, 8, 128], P('leaf', 'row', None, None, None, 'col'), may hold values from -0.09375 to 0.09375
- mid_coupling: bfloat16 [4, 8, 2, 4, 128, 4, 16, 128], P('leaf', 'row', None, None, None, 'col'), may hold values from -0.0625 to 0.0625
- leaf_targets: int32 [4, 8, 4, 6], P('leaf', 'row'), may hold values from 0 to 7, as said below
- leaf_counts: int32 [4, 8, 4], P('leaf', 'row'), may hold values from 1 to 6, as said below
- mid_targets: int32 [4, 8, 2, 4], P('leaf', 'row'), may hold values from 0 to 3, as said below
- mid_counts: int32 [4, 8, 2], P('leaf', 'row'), may hold values from 1 to 4, as said below
Outputs:
- leaf_solution: float32 [4, 8, 4, 1, 128, 256], P('leaf', 'row', 'col')
- mid_solution: float32 [4, 8, 4, 1, 128, 256], P('leaf', 'row', 'col')
- top_solution: float32 [4, 8, 4, 1, 128, 256], P('leaf', 'row', 'col')
The draws below stay inside these ranges and needn't reach their ends.
Inputs may be any that keep to these rules, and one draw needn't show every extreme that they name: `leaf_inverse`: every inverse is zero above its diagonal. `mid_inverse`: zero above the diagonal. `top_inverse`: zero above the diagonal. `leaf_targets`: live slots of one owner row and source are distinct and name a middle tile only when that middle separator is the source's ancestor (i div 2 == k div 2). `leaf_counts`: never more than the owner row's allowed targets for that source; 6 is reached in every draw. `mid_targets`: live slots of one owner row and source are distinct. `mid_counts`: 4 is reached in every draw.
All inputs are finite; a program needn't handle non-finite values.
Results may differ from the reference program's by a relative error of at most 0.034.
Values may be sent and summed in bfloat16 or wider, within the bound.
A program may use at most 128 MiB of HBM per device.

```python
import jax
import jax.numpy as jnp
from jax import lax

TILE_ROWS = 128
RHS_COLS = 256
TILES_DEV = 1
LEAF_SLOTS = 6
MID_SLOTS = 4
LEAF_TILES = 32
MID_TILES = 64
TOP_TILES = 128
N_LEAF = 4
N_ROW = 8
N_COL = 4


def factor_positions(span_leaves):
    grid_rows = span_leaves * N_ROW
    leaf_ids = jnp.arange(N_LEAF, dtype=jnp.int32).reshape(-1, 1, 1, 1, 1, 1, 1)
    row_ids = jnp.arange(N_ROW, dtype=jnp.int32).reshape(1, -1, 1, 1, 1, 1, 1)
    local_row = jnp.arange(N_COL * TILES_DEV, dtype=jnp.int32).reshape(1, 1, -1, 1, 1, 1, 1)
    inner_row = jnp.arange(TILE_ROWS, dtype=jnp.int32).reshape(1, 1, 1, -1, 1, 1, 1)
    col_ids = jnp.arange(N_COL, dtype=jnp.int32).reshape(1, 1, 1, 1, -1, 1, 1)
    local_col = jnp.arange(grid_rows * TILES_DEV, dtype=jnp.int32).reshape(1, 1, 1, 1, 1, -1, 1)
    inner_col = jnp.arange(TILE_ROWS, dtype=jnp.int32).reshape(1, 1, 1, 1, 1, 1, -1)
    group_row = leaf_ids % span_leaves * N_ROW + row_ids
    tile_row = (local_row % TILES_DEV * grid_rows + group_row) * N_COL + local_row // TILES_DEV
    tile_col = (local_col % TILES_DEV * grid_rows + local_col // TILES_DEV) * N_COL + col_ids
    entry_row = tile_row * TILE_ROWS + inner_row
    entry_col = tile_col * TILE_ROWS + inner_col
    full_shape = (N_LEAF, N_ROW, N_COL * TILES_DEV, TILE_ROWS, N_COL, grid_rows * TILES_DEV, TILE_ROWS)
    return (jnp.broadcast_to(entry_row, full_shape), jnp.broadcast_to(entry_col, full_shape))


def assemble_factor(entry_row, entry_col, lower, diagonal, order):
    below = jnp.where(entry_row == entry_col, diagonal, 0.0)
    return jnp.where(entry_row > entry_col, lower * order ** (-0.5), below).astype(jnp.bfloat16)


def draw_leaf_inverse(key, part):
    key = jax.random.fold_in(key, 11)
    entry_row, entry_col = factor_positions(1)
    lower_key, diag_key = jax.random.split(key)
    lower = jax.random.normal(lower_key, entry_row.shape, jnp.float32)
    diagonal = jax.random.uniform(diag_key, entry_row.shape, jnp.float32, 0.5, 1.5)
    return assemble_factor(entry_row, entry_col, lower, diagonal, LEAF_TILES * TILE_ROWS)


def draw_mid_inverse(key, part):
    key = jax.random.fold_in(key, 12)
    entry_row, entry_col = factor_positions(2)
    lower_key, diag_key = jax.random.split(key)
    lower = jax.random.normal(lower_key, entry_row.shape, jnp.float32)
    diagonal = jax.random.uniform(diag_key, entry_row.shape, jnp.float32, 0.5, 1.5)
    return assemble_factor(entry_row, entry_col, lower, diagonal, MID_TILES * TILE_ROWS)


def draw_top_inverse(key, part):
    key = jax.random.fold_in(key, 13)
    entry_row, entry_col = factor_positions(4)
    lower_key, diag_key = jax.random.split(key)
    lower = jax.random.normal(lower_key, entry_row.shape, jnp.float32)
    diagonal = jax.random.uniform(diag_key, entry_row.shape, jnp.float32, 0.5, 1.5)
    return assemble_factor(entry_row, entry_col, lower, diagonal, TOP_TILES * TILE_ROWS)


def draw_leaf_counts(key, part):
    key = jax.random.fold_in(key, 21)
    count_key, leaf_key, row_key, pair_key = jax.random.split(key, 4)
    local_top = N_COL * TILES_DEV
    leaf_ids = jnp.arange(N_LEAF, dtype=jnp.int32).reshape(-1, 1, 1)
    row_ids = jnp.arange(N_ROW, dtype=jnp.int32).reshape(1, -1, 1)
    source_ids = jnp.arange(N_LEAF, dtype=jnp.int32).reshape(1, 1, -1)
    allowed = jnp.where(leaf_ids // 2 == source_ids // 2, 2 * local_top, local_top)
    upper = jnp.minimum(allowed, LEAF_SLOTS)
    counts = jax.random.randint(count_key, (N_LEAF, N_ROW, N_LEAF), 1, upper + 1)
    chosen_leaf = jax.random.randint(leaf_key, (), 0, N_LEAF)
    chosen_row = jax.random.randint(row_key, (), 0, N_ROW)
    chosen_source = 2 * (chosen_leaf // 2) + jax.random.randint(pair_key, (), 0, 2)
    full_slot = (leaf_ids == chosen_leaf) & (row_ids == chosen_row) & (source_ids == chosen_source)
    return jnp.where(full_slot, LEAF_SLOTS, counts).astype(jnp.int32)


def draw_leaf_targets(key, part):
    key = jax.random.fold_in(key, 22)
    local_top = N_COL * TILES_DEV
    candidates = jnp.arange(2 * local_top, dtype=jnp.int32).reshape(1, 1, 1, -1)
    leaf_ids = jnp.arange(N_LEAF, dtype=jnp.int32).reshape(-1, 1, 1, 1)
    source_ids = jnp.arange(N_LEAF, dtype=jnp.int32).reshape(1, 1, -1, 1)
    scores = jax.random.randint(key, (N_LEAF, N_ROW, N_LEAF, 2 * local_top), 0, 1048576) * 64 + candidates
    banned = (candidates < local_top) & (leaf_ids // 2 != source_ids // 2)
    scores = scores + jnp.where(banned, 134217728, 0)
    return jnp.argsort(scores, axis=-1)[..., :LEAF_SLOTS].astype(jnp.int32)


def draw_mid_counts(key, part):
    key = jax.random.fold_in(key, 23)
    count_key, leaf_key, row_key, pair_key = jax.random.split(key, 4)
    leaf_ids = jnp.arange(N_LEAF, dtype=jnp.int32).reshape(-1, 1, 1)
    row_ids = jnp.arange(N_ROW, dtype=jnp.int32).reshape(1, -1, 1)
    source_ids = jnp.arange(N_LEAF // 2, dtype=jnp.int32).reshape(1, 1, -1)
    counts = jax.random.randint(count_key, (N_LEAF, N_ROW, N_LEAF // 2), 1, MID_SLOTS + 1)
    chosen_leaf = jax.random.randint(leaf_key, (), 0, N_LEAF)
    chosen_row = jax.random.randint(row_key, (), 0, N_ROW)
    chosen_source = jax.random.randint(pair_key, (), 0, N_LEAF // 2)
    full_slot = (leaf_ids == chosen_leaf) & (row_ids == chosen_row) & (source_ids == chosen_source)
    return jnp.where(full_slot, MID_SLOTS, counts).astype(jnp.int32)


def draw_mid_targets(key, part):
    key = jax.random.fold_in(key, 24)
    local_top = N_COL * TILES_DEV
    candidates = jnp.arange(local_top, dtype=jnp.int32).reshape(1, 1, 1, -1)
    scores = jax.random.randint(key, (N_LEAF, N_ROW, N_LEAF // 2, local_top), 0, 1048576) * 64 + candidates
    return jnp.argsort(scores, axis=-1)[..., :MID_SLOTS].astype(jnp.int32)


def block_scale(stream_key, dims, cuts, low, top_value):
    level, own = 1.0, jax.random.fold_in(stream_key, 6)
    for axis_at, blocks in cuts:
        heights = jnp.exp(jax.random.uniform(jax.random.fold_in(own, axis_at), (blocks,), jnp.float32, low / len(cuts), top_value / len(cuts)))
        level = level * jnp.repeat(heights, dims[axis_at] // blocks).reshape([-1 if axis == axis_at else 1 for axis in range(len(dims))])
    return level


def centred(key, dims, width, reach, pieces=(), kind=jnp.bfloat16):
    entries = jax.random.normal(key, dims, jnp.float32) * width
    if len(pieces) > 0:
        entries = block_scale(key, dims, pieces, -0.22, 0.18) * entries
    return jnp.clip(entries, min=-reach, max=reach).astype(kind)


def setup_inputs(seed: int = 0) -> dict:
    splits = jax.random.split(jax.random.key(seed), 13)
    return {
        "leaf_rhs": centred(splits[0], (N_LEAF, N_ROW, N_COL, TILES_DEV, TILE_ROWS, RHS_COLS), 1.0, 6.0, ((0, 4), (1, 8), (2, 4)), jnp.float32),
        "mid_rhs": centred(splits[1], (N_LEAF, N_ROW, N_COL, TILES_DEV, TILE_ROWS, RHS_COLS), 1.0, 6.0, ((0, 4), (1, 8), (2, 4)), jnp.float32),
        "top_rhs": centred(splits[2], (N_LEAF, N_ROW, N_COL, TILES_DEV, TILE_ROWS, RHS_COLS), 1.0, 6.0, ((0, 4), (1, 8), (2, 4)), jnp.float32),
        "leaf_inverse": draw_leaf_inverse(jax.random.fold_in(splits[12], 71), 0),
        "mid_inverse": draw_mid_inverse(jax.random.fold_in(splits[12], 71), 0),
        "top_inverse": draw_top_inverse(jax.random.fold_in(splits[12], 71), 0),
        "leaf_coupling": centred(splits[6], (N_LEAF, N_ROW, N_LEAF, LEAF_SLOTS, TILE_ROWS, N_COL, N_ROW * TILES_DEV, TILE_ROWS), (LEAF_TILES * TILE_ROWS) ** -0.5, 0.09375, ((0, 4), (1, 8), (5, 4))),
        "mid_coupling": centred(splits[7], (N_LEAF, N_ROW, N_LEAF // 2, MID_SLOTS, TILE_ROWS, N_COL, 2 * N_ROW * TILES_DEV, TILE_ROWS), (MID_TILES * TILE_ROWS) ** -0.5, 0.0625, ((0, 4), (1, 8), (5, 4))),
        "leaf_targets": draw_leaf_targets(jax.random.fold_in(splits[12], 71), 0),
        "leaf_counts": draw_leaf_counts(jax.random.fold_in(splits[12], 71), 0),
        "mid_targets": draw_mid_targets(jax.random.fold_in(splits[12], 71), 0),
        "mid_counts": draw_mid_counts(jax.random.fold_in(splits[12], 71), 0),
    }


precise = lax.Precision.HIGHEST


def vector_inputs(vector, span_leaves):
    supers = N_LEAF // span_leaves
    grid_rows = span_leaves * N_ROW
    grouped = vector.reshape(supers, grid_rows, N_COL, TILES_DEV, TILE_ROWS, RHS_COLS)
    return grouped.transpose(0, 2, 1, 3, 4, 5).reshape(supers, N_COL, grid_rows * TILES_DEV, TILE_ROWS, RHS_COLS)


def forward_block(inverse, vector, span_leaves):
    supers = N_LEAF // span_leaves
    grid_rows = span_leaves * N_ROW
    inputs = vector_inputs(vector, span_leaves).astype(jnp.float32)
    slabs = inverse.reshape(supers * grid_rows, N_COL * TILES_DEV, TILE_ROWS, N_COL, grid_rows * TILES_DEV, TILE_ROWS)
    owners = jnp.arange(supers * grid_rows, dtype=jnp.int32) // grid_rows

    def one_slab(operands):
        inverse_slab, owner_id = operands
        source = jnp.take(inputs, owner_id, axis=0)
        return jnp.einsum("qacpb,cpbn->qan", inverse_slab.astype(jnp.float32), source)

    product = lax.map(one_slab, (slabs, owners))
    return product.reshape(N_LEAF, N_ROW, N_COL, TILES_DEV, TILE_ROWS, RHS_COLS)


def backward_block(inverse, vector, span_leaves):
    supers = N_LEAF // span_leaves
    grid_rows = span_leaves * N_ROW
    slabs = inverse.reshape(supers * grid_rows, N_COL * TILES_DEV, TILE_ROWS, N_COL, grid_rows * TILES_DEV, TILE_ROWS)
    values = vector.reshape(supers * grid_rows, N_COL * TILES_DEV, TILE_ROWS, RHS_COLS)
    owners = jnp.arange(supers * grid_rows, dtype=jnp.int32) // grid_rows

    def add_slab(running, operands):
        inverse_slab, values_slab, owner_id = operands
        contrib = jnp.einsum("qacpb,qan->cpbn", inverse_slab.astype(jnp.float32), values_slab.astype(jnp.float32))
        return running.at[owner_id].add(contrib), None

    zeros_init = jnp.zeros((supers, N_COL, grid_rows * TILES_DEV, TILE_ROWS, RHS_COLS), jnp.float32)
    running, _ = lax.scan(add_slab, zeros_init, (slabs, values, owners))
    shaped = running.reshape(supers, N_COL, grid_rows, TILES_DEV, TILE_ROWS, RHS_COLS).transpose(0, 2, 1, 3, 4, 5)
    return shaped.reshape(N_LEAF, N_ROW, N_COL, TILES_DEV, TILE_ROWS, RHS_COLS)


def couple_forward(coupling, targets, counts, solved, span_leaves, local_tiles):
    sources = N_LEAF // span_leaves
    slot_count = targets.shape[-1]
    inputs = vector_inputs(solved, span_leaves).astype(jnp.float32)
    slabs = coupling.reshape(N_LEAF * N_ROW, sources, slot_count, TILE_ROWS, N_COL, span_leaves * N_ROW * TILES_DEV, TILE_ROWS)
    target_rows = targets.reshape(N_LEAF * N_ROW, sources, slot_count)
    count_rows = counts.reshape(N_LEAF * N_ROW, sources)

    def one_owner(operands):
        coupling_slab, target, live_count = operands
        partial_value = jnp.einsum("kiacpb,kcpbn->kian", coupling_slab.astype(jnp.float32), inputs)
        live_slots = jnp.arange(slot_count, dtype=jnp.int32)[None, :] < live_count[:, None]
        matches = target[None] == jnp.arange(local_tiles, dtype=jnp.int32)[:, None, None]
        select = (matches & live_slots[None]).astype(jnp.float32)
        return jnp.einsum("vki,kian->van", select, partial_value, precision=precise)

    return lax.map(one_owner, (slabs, target_rows, count_rows))


def couple_backward(coupling, targets, counts, ancestors, span_leaves):
    sources = N_LEAF // span_leaves
    slot_count = targets.shape[-1]
    grid_rows = span_leaves * N_ROW
    slabs = coupling.reshape(N_LEAF * N_ROW, sources, slot_count, TILE_ROWS, N_COL, grid_rows * TILES_DEV, TILE_ROWS)
    target_rows = targets.reshape(N_LEAF * N_ROW, sources, slot_count)
    count_rows = counts.reshape(N_LEAF * N_ROW, sources)

    def add_owner(running, operands):
        coupling_slab, target, live_count, local_values = operands
        live_slots = jnp.arange(slot_count, dtype=jnp.int32)[None, :] < live_count[:, None]
        chosen = jnp.take(local_values, target, axis=0) * live_slots[:, :, None, None].astype(local_values.dtype)
        contrib = jnp.einsum("kiacpb,kian->kcpbn", coupling_slab.astype(jnp.float32), chosen.astype(jnp.float32))
        return running + contrib, None

    zeros_init = jnp.zeros((sources, N_COL, grid_rows * TILES_DEV, TILE_ROWS, RHS_COLS), jnp.float32)
    running, _ = lax.scan(add_owner, zeros_init, (slabs, target_rows, count_rows, ancestors))
    shaped = running.reshape(sources, N_COL, grid_rows, TILES_DEV, TILE_ROWS, RHS_COLS).transpose(0, 2, 1, 3, 4, 5)
    return shaped.reshape(N_LEAF, N_ROW, N_COL, TILES_DEV, TILE_ROWS, RHS_COLS)


def reference(leaf_rhs, mid_rhs, top_rhs, leaf_inverse, mid_inverse, top_inverse, leaf_coupling, mid_coupling, leaf_targets, leaf_counts, mid_targets, mid_counts):
    vector_shape = leaf_rhs.shape
    local_tiles = N_COL * TILES_DEV
    leaf_input = leaf_rhs.astype(jnp.bfloat16)
    leaf_forward = forward_block(leaf_inverse, leaf_input, 1)
    leaf_solved = leaf_forward.astype(jnp.bfloat16)
    leaf_update = couple_forward(leaf_coupling, leaf_targets, leaf_counts, leaf_solved, 1, 2 * local_tiles)
    mid_input = (mid_rhs - leaf_update[:, :local_tiles].reshape(vector_shape)).astype(jnp.bfloat16)
    mid_forward = forward_block(mid_inverse, mid_input, 2)
    mid_solved = mid_forward.astype(jnp.bfloat16)
    mid_update = couple_forward(mid_coupling, mid_targets, mid_counts, mid_solved, 2, local_tiles)
    top_input = (top_rhs - leaf_update[:, local_tiles:].reshape(vector_shape) - mid_update.reshape(vector_shape)).astype(jnp.bfloat16)
    top_forward = forward_block(top_inverse, top_input, 4)
    top_solution = backward_block(top_inverse, top_forward.astype(jnp.bfloat16), 4)
    top_back = top_solution.astype(jnp.bfloat16).reshape(N_LEAF * N_ROW, local_tiles, TILE_ROWS, RHS_COLS)
    mid_return = couple_backward(mid_coupling, mid_targets, mid_counts, top_back, 2)
    mid_solution = backward_block(mid_inverse, (mid_forward - mid_return).astype(jnp.bfloat16), 2)
    mid_back = mid_solution.astype(jnp.bfloat16).reshape(N_LEAF * N_ROW, local_tiles, TILE_ROWS, RHS_COLS)
    ancestors = jnp.concatenate([mid_back, top_back], axis=1)
    leaf_return = couple_backward(leaf_coupling, leaf_targets, leaf_counts, ancestors, 1)
    leaf_solution = backward_block(leaf_inverse, (leaf_forward - leaf_return).astype(jnp.bfloat16), 1)
    return leaf_solution, mid_solution, top_solution
```

```python
import functools

import jax
import jax.numpy as jnp
from jax import lax
from jax.experimental import pallas as pl
from jax.experimental.pallas import tpu as pltpu
from jax.sharding import PartitionSpec as P

MESH = pl.DeviceIdType.MESH
TILE = 128
GROUP = 4 * TILE
CHAINS = 2
BF = jnp.bfloat16
F32 = jnp.float32


def kernel(
    width,
    leaf_rhs,
    mid_rhs,
    top_rhs,
    leaf_inv,
    mid_inv,
    top_inv,
    leaf_cpl,
    mid_cpl,
    leaf_tgt,
    leaf_cnt,
    mid_tgt,
    mid_cnt,
    leaf_out,
    mid_out,
    top_out,
    st_li,
    st_lc0,
    st_lc1,
    st_16a,
    st_16b,
    st_ti,
    wl,
    wm,
    wt,
    gm,
    gt,
    hm,
    x1,
    x2,
    x3,
    x4,
    x5,
    pf,
    xs,
    xr,
    top_part,
    yt,
    sib_s,
    pl_s,
    sib_r0,
    sib_r1,
    sib_r2,
    pl_r0,
    pl_r1,
    pl_r3,
    pl_r4,
    pl_r5,
    own,
    top_acc,
    lf,
    mf,
    w_sem,
    ag_rx,
    ag_rxs,
    ag_tx,
    ag_txs,
    x_rx,
    x_tx,
    rs_rx,
    rs_rxs,
    rs_tx,
    rs_txs,
):
    y = lax.axis_index("leaf")
    row = lax.axis_index("row")
    c = lax.axis_index("col")
    z, e = lax.div(row, 2), lax.rem(row, 2)
    eo = 1 - e
    half = lax.div(y, 2)
    par = lax.rem(y, 2)

    def partners(a):
        near = a + 1 - 2 * lax.rem(a, 2)
        return [a, near, lax.rem(a + 2, 4), lax.rem(near + 2, 4)]

    ys, zs, cs = partners(y), partners(z), partners(c)
    pars = [par, 1 - par]
    sibling = (y, z * 2 + eo, c)

    def plane(dy, dz):
        return (ys[dy], zs[dz] * 2 + e, c)

    srcs = [2 * half, 2 * half + 1, 2 * (1 - half), 2 * (1 - half) + 1]
    fetch = {
        "li": pltpu.make_async_copy(leaf_inv, st_li, w_sem.at[0]),
        "lc0": pltpu.make_async_copy(leaf_cpl.at[srcs[0]], st_lc0, w_sem.at[1]),
        "lc1": pltpu.make_async_copy(leaf_cpl.at[srcs[1]], st_lc1, w_sem.at[2]),
        "mi": pltpu.make_async_copy(mid_inv, st_16a, w_sem.at[3]),
        "lc2": pltpu.make_async_copy(leaf_cpl.at[srcs[2]], st_lc0, w_sem.at[4]),
        "lc3": pltpu.make_async_copy(leaf_cpl.at[srcs[3]], st_lc1, w_sem.at[5]),
        "hm0": pltpu.make_async_copy(mid_cpl.at[0], st_16b, w_sem.at[6]),
        "hm1": pltpu.make_async_copy(mid_cpl.at[1], st_16a, w_sem.at[7]),
        "ti": pltpu.make_async_copy(top_inv, st_ti, w_sem.at[8]),
    }
    for name in ("li", "lc0", "lc1", "mi", "hm0", "ti"):
        fetch[name].start()

    def by_core(x, first, core):
        at = [(first + 2 * k + core) * TILE for k in range(4)]
        return jnp.concatenate([x[:, a : a + TILE] for a in at], axis=1)

    def lay_inverse(name, stage, dst, groups):
        fetch[name].wait()
        for q in range(4):
            rows = slice(q * TILE, (q + 1) * TILE)
            x = stage[rows].reshape(TILE, groups * 8 * TILE)
            for g in range(groups):
                for core in range(2):
                    dst[core, g, rows, :] = by_core(x, g * 8, core)

    def find_slot(targets, counts, k, v, slots):
        at, live = jnp.int32(0), jnp.int32(0)
        for m in range(slots):
            hit = jnp.logical_and(targets[k, m] == v, m < counts[k])
            at = jnp.where(hit, m, at)
            live = jnp.where(hit, 1, live)
        return at, live

    def lay_slot(x, live, width_tiles):
        x = x.reshape(TILE, width_tiles * TILE)
        return x * jnp.full(x.shape, live.astype(F32), F32).astype(BF)

    def lay_leaf_coupling(j):
        k = srcs[j]
        fetch[f"lc{j}"].wait()
        for v in range(0 if j < 2 else 4, 8):
            at, live = find_slot(leaf_tgt, leaf_cnt, k, v, 6)
            x = lay_slot((st_lc0, st_lc1)[j % 2][at], live, 8)
            rows = slice(v % 4 * TILE, (v % 4 + 1) * TILE)
            for core in range(2):
                if v < 4:
                    gm[core, j, rows, :] = by_core(x, 0, core)
                else:
                    gt[core, k, rows, :] = by_core(x, 0, core)
        if j < 2:
            fetch[f"lc{j + 2}"].start()

    def lay_mid_inverse():
        fetch["mi"].wait()
        for q in range(4):
            rows = slice(q * TILE, (q + 1) * TILE)
            x = st_16a[q].reshape(TILE, 16 * TILE)
            for g in range(2):
                for core in range(2):
                    wm[core, g, rows, :] = by_core(x, g * 8, core)
        fetch["hm1"].start()

    def lay_mid_coupling(k):
        fetch[f"hm{k}"].wait()
        for v in range(4):
            at, live = find_slot(mid_tgt, mid_cnt, k, v, 4)
            x = lay_slot((st_16b, st_16a)[k][at], live, 16)
            rows = slice(v * TILE, (v + 1) * TILE)
            for g in range(2):
                for core in range(2):
                    hm[core, 2 * k + g, rows, :] = by_core(x, g * 8, core)

    tasks = {
        0: [lambda: lay_inverse("li", st_li, wl, 1)],
        1: [lambda: lay_leaf_coupling(0), lambda: lay_leaf_coupling(1)],
        2: [lay_mid_inverse, lambda: lay_leaf_coupling(2)],
        3: [lambda: lay_leaf_coupling(3), lambda: lay_mid_coupling(0)],
        4: [lambda: lay_mid_coupling(1)],
        5: [lambda: lay_inverse("ti", st_ti, wt, 4)],
    }

    barrier = pltpu.get_barrier_semaphore()
    reached = [sibling] + [plane(a, b) for a in range(4) for b in range(4) if a or b]
    reached += [(y, row, cs[k]) for k in range(1, 4)]
    for device in reached:
        pl.semaphore_signal(barrier, inc=1, device_id=device, device_id_type=MESH)
    pl.semaphore_wait(barrier, len(reached))

    def remote(src, dst, tx, rx, device):
        return pltpu.make_async_remote_copy(
            src_ref=src, dst_ref=dst, send_sem=tx, recv_sem=rx, device_id=device, device_id_type=MESH
        )

    def chain(h):
        sent = []
        cols = slice(h * width, (h + 1) * width)

        def drain():
            for ref, sem in sent:
                remote(ref, ref, sem, sem, sibling).wait_send()
            sent.clear()

        def arrived(ref, sem):
            remote(ref, ref, sem, sem, sibling).wait_recv()

        def gather_send(ph, x, at, value, dys):
            mine = x.at[h, e, at[0], pl.ds(z * TILE, TILE)]
            x[h, e, at[0], pl.ds(z * TILE, TILE), :] = value
            for dy in dys:
                for dz in (2, 1, 3, 0):
                    if dy or dz:
                        remote(mine, mine, ag_tx.at[ph, h, dy], ag_rx.at[ph, h, dy], plane(dy, dz)).start()
                tiles = 4 if dy else 3
                sent.append((x.at[h, 0, 0, pl.ds(0, tiles * TILE)], ag_tx.at[ph, h, dy]))

        def gather_forward(ph, x, at, dy):
            tiles = 4 if dy else 3
            arrived(x.at[h, e, at[dy], pl.ds(0, tiles * TILE)], ag_rx.at[ph, h, dy])
            block = x.at[h, e, at[dy]]
            remote(block, block, ag_txs.at[ph, h, dy], ag_rxs.at[ph, h, dy], sibling).start()
            sent.append((block, ag_txs.at[ph, h, dy]))

        def gather_done(ph, x, at, dy):
            arrived(x.at[h, eo, at[dy]], ag_rxs.at[ph, h, dy])

        def products(w, wat, x, at, core, dys):
            total = None
            for dy in dys:
                part = jnp.dot(w[core, wat[dy]], x[h, core, at[dy]], preferred_element_type=F32)
                total = part if total is None else total + part
            return total

        def gathered_product(ph, w, wat, x, at, dys):
            for dy in dys:
                gather_forward(ph, x, at, dy)
            total = products(w, wat, x, at, e, dys)
            for dy in dys:
                gather_done(ph, x, at, dy)
            return total + products(w, wat, x, at, eo, dys)

        def column_send(ph, total):
            for q in range(4):
                tile = total[q * TILE : (q + 1) * TILE]
                pf[h, q] = tile
                xs[ph, h, q] = tile.astype(BF)
            for dc in (2, 1, 3):
                remote(
                    xs.at[ph, h, cs[dc]], xr.at[ph, h, dc - 1], x_tx.at[ph, h], x_rx.at[ph, h], (y, row, cs[dc])
                ).start()
            sent.append((xs.at[ph, h, pl.ds(0, 3)], x_tx.at[ph, h]))

        def column_sum(ph):
            arrived(xr.at[ph, h], x_rx.at[ph, h])
            total = pf[h, c]
            for k in range(3):
                total = total + xr[ph, h, k].astype(F32)
            return total

        def row_send(ph, value):
            mine = yt.at[ph, h, c]
            yt[ph, h, c] = value
            for dc in (2, 1, 3):
                remote(mine, mine, x_tx.at[5 + ph, h], x_rx.at[5 + ph, h], (y, row, cs[dc])).start()
            sent.append((yt.at[ph, h, pl.ds(0, 3)], x_tx.at[5 + ph, h]))

        def row_tiles(ph):
            arrived(yt.at[ph, h, pl.ds(0, 3)], x_rx.at[5 + ph, h])
            return jnp.concatenate([yt[ph, h, q] for q in range(4)], axis=1)

        def group_send(ph, piece, s_at, sib_r, r_at, pl_r, dys):
            for k, dy in enumerate(dys):
                sib_s[s_at, h, dy] = piece(0, dy).astype(BF)
                remote(
                    sib_s.at[s_at, h, dy], sib_r.at[r_at, h, dy], rs_txs.at[ph, h, dy], rs_rxs.at[ph, h, dy], sibling
                ).start()
                sent.append((sib_s.at[s_at, h, dy], rs_txs.at[ph, h, dy]))
            for dy in dys:
                total = piece(1, dy)
                arrived(sib_r.at[r_at, h, dy], rs_rxs.at[ph, h, dy])
                total = total + sib_r[r_at, h, dy].astype(F32)
                for k in range(4):
                    tile = total[:, k * TILE : (k + 1) * TILE]
                    pl_s[s_at, h, dy * 4 + k] = tile.astype(BF)
                    if dy == 0:
                        own[h, k] = tile
                for dz in (2, 1, 3, 0):
                    if dy or dz:
                        remote(
                            pl_s.at[s_at, h, dy * 4 + zs[dz]],
                            pl_r.at[h, dy * 4 + dz],
                            rs_tx.at[ph, h, dy],
                            rs_rx.at[ph, h],
                            plane(dy, dz),
                        ).start()
                tiles = 4 if dy else 3
                sent.append((pl_s.at[s_at, h, pl.ds(0, tiles)], rs_tx.at[ph, h, dy]))

        def group_sum(ph, pl_r, tiles):
            arrived(pl_r.at[h, pl.ds(1, tiles)], rs_rx.at[ph, h])
            total = own[h, z]
            for k in range(1, tiles + 1):
                total = total + pl_r[h, k].astype(F32)
            return total

        zero = [0]
        far = (2, 1, 3, 0)

        gather_send(0, x1, zero, leaf_rhs[:, cols].astype(BF), (0,))
        yield
        column_send(0, gathered_product(0, wl, zero, x1, zero, (0,)))
        yield
        drain()
        forward = column_sum(0)
        gather_send(1, x2, ys, forward.astype(BF), (1, 0, 2, 3))
        lf[h] = forward.T
        yield
        column_send(1, gathered_product(1, gm, pars, x2, ys, (0, 1)))
        yield
        drain()
        gather_send(2, x3, pars, (mid_rhs[:, cols] - column_sum(1)).astype(BF), (1, 0))
        for dy in (3, 2):
            gather_forward(1, x2, ys, dy)
        yield
        column_send(2, gathered_product(2, wm, pars, x3, pars, (0, 1)))
        for dy in (3, 2):
            gather_done(1, x2, ys, dy)
        top_part[h] = products(gt, ys, x2, ys, e, far) + products(gt, ys, x2, ys, eo, far)
        yield
        drain()
        forward = column_sum(2)
        gather_send(3, x4, ys, forward.astype(BF), far)
        mf[h] = forward.T
        yield
        column_send(3, gathered_product(3, hm, ys, x4, ys, (0, 1, 3, 2)) + top_part[h])
        yield
        drain()
        gather_send(4, x5, ys, (top_rhs[:, cols] - column_sum(3)).astype(BF), far)
        yield
        column_send(4, gathered_product(4, wt, ys, x5, ys, (0, 1, 3, 2)))
        yield
        drain()
        row_send(0, column_sum(4).T.astype(BF))
        yield

        def both(w, wat, values):
            def piece(mine, dy):
                return jnp.dot(values, w[e if mine else eo, wat[dy]], preferred_element_type=F32)

            return piece

        values = row_tiles(0)
        group_send(0, both(wt, ys, values), 0, sib_r0, 0, pl_r0, far)
        yield
        drain()
        solution_t = group_sum(0, pl_r0, 15)
        row_send(1, solution_t.astype(BF))
        top_out[:, cols] = solution_t.T
        yield
        values = row_tiles(1)
        group_send(1, both(hm, ys, values), 1, sib_r0, 1, pl_r1, far)
        part = both(gt, ys, values)
        for mine in range(2):
            for dy in range(2):
                top_acc[h, mine, dy] = part(mine, dy)
        yield
        drain()
        row_send(2, (mf[h] - group_sum(1, pl_r1, 15)).astype(BF))
        group_send(2, part, 0, sib_r0, 2, pl_r4, (2, 3))
        yield
        values = row_tiles(2)
        group_send(3, both(wm, pars, values), 1, sib_r1, 0, pl_r3, (1, 0))
        yield
        drain()
        solution_t = group_sum(3, pl_r3, 7)
        row_send(3, solution_t.astype(BF))
        mid_out[:, cols] = solution_t.T
        arrived(pl_r4.at[h, pl.ds(8, 8)], rs_rx.at[2, h])
        late = lf[h]
        for k in range(8, 16):
            late = late - pl_r4[h, k].astype(F32)
        lf[h] = late
        yield
        values = row_tiles(3)
        mid_piece = both(gm, pars, values)
        group_send(
            4, lambda mine, dy: mid_piece(mine, dy) + top_acc[h, mine, dy], 0, sib_r1, 1, pl_r4, (1, 0)
        )
        yield
        drain()
        row_send(4, (lf[h] - group_sum(4, pl_r4, 7)).astype(BF))
        yield
        values = row_tiles(4)
        group_send(5, both(wl, zero, values), 1, sib_r2, 0, pl_r5, (0,))
        yield
        drain()
        leaf_out[:, cols] = group_sum(5, pl_r5, 3).T
        drain()

    running = [chain(h) for h in range(CHAINS)]
    step = 0
    while running:
        alive = []
        for g in running:
            if next(g, "end") != "end":
                alive.append(g)
        running = alive
        for task in tasks.get(step, ()):
            task()
        step += 1


def shards(
    leaf_rhs,
    mid_rhs,
    top_rhs,
    leaf_inverse,
    mid_inverse,
    top_inverse,
    leaf_coupling,
    mid_coupling,
    leaf_targets,
    leaf_counts,
    mid_targets,
    mid_counts,
):
    shape = leaf_rhs.shape
    rhs = shape[-1]
    n = rhs // CHAINS
    h = CHAINS
    vmem = pl.BlockSpec(memory_space=pltpu.VMEM)
    smem = pl.BlockSpec(memory_space=pltpu.SMEM)
    hbm = pl.BlockSpec(memory_space=pl.ANY)
    out = jax.ShapeDtypeStruct((TILE, rhs), F32)
    dma = pltpu.SemaphoreType.DMA
    weights = [pltpu.VMEM((2, k, GROUP, GROUP), BF) for k in (1, 2, 4, 2, 4, 4)]
    vectors = [pltpu.VMEM((h, 2, k, GROUP, n), BF) for k in (1, 4, 2, 4, 4)]
    outs = pl.pallas_call(
        functools.partial(kernel, n),
        out_shape=(out, out, out),
        in_specs=[vmem] * 3 + [hbm] * 5 + [smem] * 4,
        out_specs=(vmem, vmem, vmem),
        scratch_shapes=[
            pltpu.VMEM((GROUP, 8, TILE), BF),
            pltpu.VMEM((6, TILE, 8, TILE), BF),
            pltpu.VMEM((6, TILE, 8, TILE), BF),
            pltpu.VMEM((4, TILE, 16, TILE), BF),
            pltpu.VMEM((4, TILE, 16, TILE), BF),
            pltpu.VMEM((GROUP, 32, TILE), BF),
            *weights,
            *vectors,
            pltpu.VMEM((h, 4, TILE, n), F32),
            pltpu.VMEM((5, h, 4, TILE, n), BF),
            pltpu.VMEM((5, h, 3, TILE, n), BF),
            pltpu.VMEM((h, GROUP, n), F32),
            pltpu.VMEM((5, h, 4, n, TILE), BF),
            pltpu.VMEM((2, h, 4, n, GROUP), BF),
            pltpu.VMEM((2, h, 16, n, TILE), BF),
            pltpu.VMEM((3, h, 4, n, GROUP), BF),
            pltpu.VMEM((2, h, 2, n, GROUP), BF),
            pltpu.VMEM((1, h, 1, n, GROUP), BF),
            pltpu.VMEM((h, 16, n, TILE), BF),
            pltpu.VMEM((h, 16, n, TILE), BF),
            pltpu.VMEM((h, 8, n, TILE), BF),
            pltpu.VMEM((h, 16, n, TILE), BF),
            pltpu.VMEM((h, 4, n, TILE), BF),
            pltpu.VMEM((h, 4, n, TILE), F32),
            pltpu.VMEM((h, 2, 2, n, GROUP), F32),
            pltpu.VMEM((h, n, TILE), F32),
            pltpu.VMEM((h, n, TILE), F32),
            dma((9,)),
            dma((5, h, 4)),
            dma((5, h, 4)),
            dma((5, h, 4)),
            dma((5, h, 4)),
            dma((10, h)),
            dma((10, h)),
            dma((6, h)),
            dma((6, h, 4)),
            dma((6, h, 4)),
            dma((6, h, 4)),
        ],
        compiler_params=pltpu.CompilerParams(
            collective_id=0, has_side_effects=True, vmem_limit_bytes=62 * 2**20
        ),
        cost_estimate=pl.CostEstimate(flops=9_200_000_000, bytes_accessed=19_000_000, transcendentals=0),
    )(
        leaf_rhs.reshape(TILE, rhs),
        mid_rhs.reshape(TILE, rhs),
        top_rhs.reshape(TILE, rhs),
        leaf_inverse.reshape(GROUP, 8, TILE),
        mid_inverse.reshape(4, TILE, 16, TILE),
        top_inverse.reshape(GROUP, 32, TILE),
        leaf_coupling.reshape(4, 6, TILE, 8, TILE),
        mid_coupling.reshape(2, 4, TILE, 16, TILE),
        leaf_targets[0, 0],
        leaf_counts[0, 0],
        mid_targets[0, 0],
        mid_counts[0, 0],
    )
    return tuple(o.reshape(shape) for o in outs)


def solution(mesh):
    vector = P("leaf", "row", "col", None, None, None)
    inverse = P("leaf", "row", None, None, "col", None, None)
    coupling = P("leaf", "row", None, None, None, "col", None, None)
    placed = (
        vector,
        vector,
        vector,
        inverse,
        inverse,
        inverse,
        coupling,
        coupling,
        P("leaf", "row", None, None),
        P("leaf", "row", None),
        P("leaf", "row", None, None),
        P("leaf", "row", None),
    )
    return jax.shard_map(
        shards, mesh=mesh, in_specs=placed, out_specs=(vector, vector, vector), check_vma=False
    )
```

```python
import functools

import jax
import jax.numpy as jnp
from jax import lax
from jax.experimental import pallas as pl
from jax.experimental.pallas import tpu as pltpu
from jax.sharding import PartitionSpec as P

MESH = pl.DeviceIdType.MESH
TILE = 128
GROUP = 4 * TILE
CHAINS = 2
BF = jnp.bfloat16
F32 = jnp.float32


def kernel(
    width,
    leaf_rhs,
    mid_rhs,
    top_rhs,
    leaf_inv,
    mid_inv,
    top_inv,
    leaf_cpl,
    mid_cpl,
    leaf_tgt,
    leaf_cnt,
    mid_tgt,
    mid_cnt,
    leaf_out,
    mid_out,
    top_out,
    st_li,
    st_lc0,
    st_lc1,
    st_16a,
    st_16b,
    st_ti,
    wl,
    wm,
    wt,
    gm,
    gt,
    hm,
    x1,
    x2,
    x3,
    x4,
    x5,
    pf,
    xs,
    xr,
    top_part,
    yt,
    sib_s,
    pl_s,
    sib_r0,
    sib_r1,
    sib_r2,
    pl_r0,
    pl_r1,
    pl_r3,
    pl_r4,
    pl_r5,
    own,
    top_acc,
    lf,
    mf,
    w_sem,
    ag_rx,
    ag_rxs,
    ag_tx,
    ag_txs,
    x_rx,
    x_tx,
    rs_rx,
    rs_rxs,
    rs_tx,
    rs_txs,
):
    y = lax.axis_index("leaf")
    row = lax.axis_index("row")
    c = lax.axis_index("col")
    z, e = lax.div(row, 2), lax.rem(row, 2)
    eo = 1 - e
    half = lax.div(y, 2)
    par = lax.rem(y, 2)

    def partners(a):
        near = a + 1 - 2 * lax.rem(a, 2)
        return [a, near, lax.rem(a + 2, 4), lax.rem(near + 2, 4)]

    ys, zs, cs = partners(y), partners(z), partners(c)
    pars = [par, 1 - par]
    sibling = (y, z * 2 + eo, c)

    def plane(dy, dz):
        return (ys[dy], zs[dz] * 2 + e, c)

    srcs = [2 * half, 2 * half + 1, 2 * (1 - half), 2 * (1 - half) + 1]
    fetch = {
        "li": pltpu.make_async_copy(leaf_inv, st_li, w_sem.at[0]),
        "lc0": pltpu.make_async_copy(leaf_cpl.at[srcs[0]], st_lc0, w_sem.at[1]),
        "lc1": pltpu.make_async_copy(leaf_cpl.at[srcs[1]], st_lc1, w_sem.at[2]),
        "mi": pltpu.make_async_copy(mid_inv, st_16a, w_sem.at[3]),
        "lc2": pltpu.make_async_copy(leaf_cpl.at[srcs[2]], st_lc0, w_sem.at[4]),
        "lc3": pltpu.make_async_copy(leaf_cpl.at[srcs[3]], st_lc1, w_sem.at[5]),
        "hm0": pltpu.make_async_copy(mid_cpl.at[0], st_16b, w_sem.at[6]),
        "hm1": pltpu.make_async_copy(mid_cpl.at[1], st_16a, w_sem.at[7]),
        "ti": pltpu.make_async_copy(top_inv, st_ti, w_sem.at[8]),
    }
    for name in ("li", "lc0", "lc1", "mi", "hm0", "ti"):
        fetch[name].start()

    def by_core(x, first, core):
        at = [(first + 2 * k + core) * TILE for k in range(4)]
        return jnp.concatenate([x[:, a : a + TILE] for a in at], axis=1)

    def lay_inverse(name, stage, dst, groups):
        fetch[name].wait()
        for q in range(4):
            rows = slice(q * TILE, (q + 1) * TILE)
            x = stage[rows].reshape(TILE, groups * 8 * TILE)
            for g in range(groups):
                for core in range(2):
                    dst[core, g, rows, :] = by_core(x, g * 8, core)

    def find_slot(targets, counts, k, v, slots):
        at, live = jnp.int32(0), jnp.int32(0)
        for m in range(slots):
            hit = jnp.logical_and(targets[k, m] == v, m < counts[k])
            at = jnp.where(hit, m, at)
            live = jnp.where(hit, 1, live)
        return at, live

    def lay_slot(x, live, width_tiles):
        x = x.reshape(TILE, width_tiles * TILE)
        return x * jnp.full(x.shape, live.astype(F32), F32).astype(BF)

    def lay_leaf_coupling(j):
        k = srcs[j]
        fetch[f"lc{j}"].wait()
        for v in range(0 if j < 2 else 4, 8):
            at, live = find_slot(leaf_tgt, leaf_cnt, k, v, 6)
            x = lay_slot((st_lc0, st_lc1)[j % 2][at], live, 8)
            rows = slice(v % 4 * TILE, (v % 4 + 1) * TILE)
            for core in range(2):
                if v < 4:
                    gm[core, j, rows, :] = by_core(x, 0, core)
                else:
                    gt[core, k, rows, :] = by_core(x, 0, core)
        if j < 2:
            fetch[f"lc{j + 2}"].start()

    def lay_mid_inverse():
        fetch["mi"].wait()
        for q in range(4):
            rows = slice(q * TILE, (q + 1) * TILE)
            x = st_16a[q].reshape(TILE, 16 * TILE)
            for g in range(2):
                for core in range(2):
                    wm[core, g, rows, :] = by_core(x, g * 8, core)
        fetch["hm1"].start()

    def lay_mid_coupling(k):
        fetch[f"hm{k}"].wait()
        for v in range(4):
            at, live = find_slot(mid_tgt, mid_cnt, k, v, 4)
            x = lay_slot((st_16b, st_16a)[k][at], live, 16)
            rows = slice(v * TILE, (v + 1) * TILE)
            for g in range(2):
                for core in range(2):
                    hm[core, 2 * k + g, rows, :] = by_core(x, g * 8, core)

    tasks = {
        0: [lambda: lay_inverse("li", st_li, wl, 1)],
        1: [lambda: lay_leaf_coupling(0), lambda: lay_leaf_coupling(1)],
        2: [lay_mid_inverse, lambda: lay_leaf_coupling(2)],
        3: [lambda: lay_leaf_coupling(3), lambda: lay_mid_coupling(0)],
        4: [lambda: lay_mid_coupling(1)],
        5: [lambda: lay_inverse("ti", st_ti, wt, 4)],
    }

    barrier = pltpu.get_barrier_semaphore()
    reached = [sibling] + [plane(0, k) for k in range(1, 4)] + [plane(k, 0) for k in range(1, 4)]
    reached += [(y, row, cs[k]) for k in range(1, 4)]
    for device in reached:
        pl.semaphore_signal(barrier, inc=1, device_id=device, device_id_type=MESH)
    pl.semaphore_wait(barrier, len(reached))

    def remote(src, dst, tx, rx, device):
        return pltpu.make_async_remote_copy(
            src_ref=src, dst_ref=dst, send_sem=tx, recv_sem=rx, device_id=device, device_id_type=MESH
        )

    def chain(h):
        sent = []
        cols = slice(h * width, (h + 1) * width)

        def drain():
            for ref, sem in sent:
                remote(ref, ref, sem, sem, sibling).wait_send()
            sent.clear()

        def arrived(ref, sem):
            remote(ref, ref, sem, sem, sibling).wait_recv()

        def gather_send(ph, x, at, value, dys):
            mine = x.at[h, e, at[0], pl.ds(z * TILE, TILE)]
            x[h, e, at[0], pl.ds(z * TILE, TILE), :] = value
            for dy in dys:
                for dz in (2, 1, 3, 0):
                    if dy or dz:
                        remote(mine, mine, ag_tx.at[ph, h, dy], ag_rx.at[ph, h, dy], plane(dy, dz)).start()
                tiles = 4 if dy else 3
                sent.append((x.at[h, 0, 0, pl.ds(0, tiles * TILE)], ag_tx.at[ph, h, dy]))

        def gather_forward(ph, x, at, dy):
            tiles = 4 if dy else 3
            arrived(x.at[h, e, at[dy], pl.ds(0, tiles * TILE)], ag_rx.at[ph, h, dy])
            block = x.at[h, e, at[dy]]
            remote(block, block, ag_txs.at[ph, h, dy], ag_rxs.at[ph, h, dy], sibling).start()
            sent.append((block, ag_txs.at[ph, h, dy]))

        def gather_done(ph, x, at, dy):
            arrived(x.at[h, eo, at[dy]], ag_rxs.at[ph, h, dy])

        def gathered_product(ph, w, wat, x, at, dys):
            def part(core, dy):
                return jnp.dot(w[core, wat[dy]], x[h, core, at[dy]], preferred_element_type=F32)

            total = None
            for dy in dys:
                gather_forward(ph, x, at, dy)
                total = part(e, dy) if total is None else total + part(e, dy)
            for dy in dys:
                gather_done(ph, x, at, dy)
                total = total + part(eo, dy)
            return total

        def column_send(ph, total):
            for q in range(4):
                tile = total[q * TILE : (q + 1) * TILE]
                pf[h, q] = tile
                xs[ph, h, q] = tile.astype(BF)
            for dc in (2, 1, 3):
                remote(
                    xs.at[ph, h, cs[dc]], xr.at[ph, h, dc - 1], x_tx.at[ph, h], x_rx.at[ph, h], (y, row, cs[dc])
                ).start()
            sent.append((xs.at[ph, h, pl.ds(0, 3)], x_tx.at[ph, h]))

        def column_sum(ph):
            arrived(xr.at[ph, h], x_rx.at[ph, h])
            total = pf[h, c]
            for k in range(3):
                total = total + xr[ph, h, k].astype(F32)
            return total

        def row_send(ph, value):
            mine = yt.at[ph, h, c]
            yt[ph, h, c] = value
            for dc in (2, 1, 3):
                remote(mine, mine, x_tx.at[5 + ph, h], x_rx.at[5 + ph, h], (y, row, cs[dc])).start()
            sent.append((yt.at[ph, h, pl.ds(0, 3)], x_tx.at[5 + ph, h]))

        def row_tiles(ph):
            arrived(yt.at[ph, h, pl.ds(0, 3)], x_rx.at[5 + ph, h])
            return jnp.concatenate([yt[ph, h, q] for q in range(4)], axis=1)

        def group_send(ph, piece, s_at, sib_r, r_at, pl_r, dys):
            for k, dy in enumerate(dys):
                sib_s[s_at, h, dy] = piece(0, dy).astype(BF)
                remote(
                    sib_s.at[s_at, h, dy], sib_r.at[r_at, h, dy], rs_txs.at[ph, h, dy], rs_rxs.at[ph, h, dy], sibling
                ).start()
                sent.append((sib_s.at[s_at, h, dy], rs_txs.at[ph, h, dy]))
            for dy in dys:
                total = piece(1, dy)
                arrived(sib_r.at[r_at, h, dy], rs_rxs.at[ph, h, dy])
                total = total + sib_r[r_at, h, dy].astype(F32)
                for k in range(4):
                    tile = total[:, k * TILE : (k + 1) * TILE]
                    pl_s[s_at, h, dy * 4 + k] = tile.astype(BF)
                    if dy == 0:
                        own[h, k] = tile
                for dz in (2, 1, 3, 0):
                    if dy or dz:
                        remote(
                            pl_s.at[s_at, h, dy * 4 + zs[dz]],
                            pl_r.at[h, dy * 4 + dz],
                            rs_tx.at[ph, h, dy],
                            rs_rx.at[ph, h],
                            plane(dy, dz),
                        ).start()
                tiles = 4 if dy else 3
                sent.append((pl_s.at[s_at, h, pl.ds(0, tiles)], rs_tx.at[ph, h, dy]))

        def group_sum(ph, pl_r, tiles):
            arrived(pl_r.at[h, pl.ds(1, tiles)], rs_rx.at[ph, h])
            total = own[h, z]
            for k in range(1, tiles + 1):
                total = total + pl_r[h, k].astype(F32)
            return total

        zero = [0]
        far = (2, 1, 3, 0)

        gather_send(0, x1, zero, leaf_rhs[:, cols].astype(BF), (0,))
        yield
        column_send(0, gathered_product(0, wl, zero, x1, zero, (0,)))
        yield
        drain()
        forward = column_sum(0)
        gather_send(1, x2, ys, forward.astype(BF), (1, 0, 2, 3))
        lf[h] = forward.T
        yield
        column_send(1, gathered_product(1, gm, pars, x2, ys, (0, 1)))
        yield
        drain()
        gather_send(2, x3, pars, (mid_rhs[:, cols] - column_sum(1)).astype(BF), (1, 0))
        for dy in (3, 2):
            gather_forward(1, x2, ys, dy)
        yield
        column_send(2, gathered_product(2, wm, pars, x3, pars, (0, 1)))
        for dy in (3, 2):
            gather_done(1, x2, ys, dy)
        total = None
        for core in (e, eo):
            for dy in far:
                part = jnp.dot(gt[core, ys[dy]], x2[h, core, ys[dy]], preferred_element_type=F32)
                total = part if total is None else total + part
        top_part[h] = total
        yield
        drain()
        forward = column_sum(2)
        gather_send(3, x4, ys, forward.astype(BF), far)
        mf[h] = forward.T
        yield
        column_send(3, gathered_product(3, hm, ys, x4, ys, (0, 1, 3, 2)) + top_part[h])
        yield
        drain()
        gather_send(4, x5, ys, (top_rhs[:, cols] - column_sum(3)).astype(BF), far)
        yield
        column_send(4, gathered_product(4, wt, ys, x5, ys, (0, 1, 3, 2)))
        yield
        drain()
        row_send(0, column_sum(4).T.astype(BF))
        yield

        def both(w, wat, values):
            def piece(mine, dy):
                return jnp.dot(values, w[e if mine else eo, wat[dy]], preferred_element_type=F32)

            return piece

        values = row_tiles(0)
        group_send(0, both(wt, ys, values), 0, sib_r0, 0, pl_r0, far)
        yield
        drain()
        solution_t = group_sum(0, pl_r0, 15)
        row_send(1, solution_t.astype(BF))
        top_out[:, cols] = solution_t.T
        yield
        values = row_tiles(1)
        group_send(1, both(hm, ys, values), 1, sib_r0, 1, pl_r1, far)
        part = both(gt, ys, values)
        for mine in range(2):
            for dy in range(2):
                top_acc[h, mine, dy] = part(mine, dy)
        yield
        drain()
        row_send(2, (mf[h] - group_sum(1, pl_r1, 15)).astype(BF))
        group_send(2, part, 0, sib_r0, 2, pl_r4, (2, 3))
        yield
        values = row_tiles(2)
        group_send(3, both(wm, pars, values), 1, sib_r1, 0, pl_r3, (1, 0))
        yield
        drain()
        solution_t = group_sum(3, pl_r3, 7)
        row_send(3, solution_t.astype(BF))
        mid_out[:, cols] = solution_t.T
        arrived(pl_r4.at[h, pl.ds(8, 8)], rs_rx.at[2, h])
        late = lf[h]
        for k in range(8, 16):
            late = late - pl_r4[h, k].astype(F32)
        lf[h] = late
        yield
        values = row_tiles(3)
        mid_piece = both(gm, pars, values)
        group_send(
            4, lambda mine, dy: mid_piece(mine, dy) + top_acc[h, mine, dy], 0, sib_r1, 1, pl_r4, (1, 0)
        )
        yield
        drain()
        row_send(4, (lf[h] - group_sum(4, pl_r4, 7)).astype(BF))
        yield
        values = row_tiles(4)
        group_send(5, both(wl, zero, values), 1, sib_r2, 0, pl_r5, (0,))
        yield
        drain()
        leaf_out[:, cols] = group_sum(5, pl_r5, 3).T
        drain()

    running = [chain(h) for h in range(CHAINS)]
    order = ((0,), (1, 2), (3, 4), (5, 6), (7, 8), (9, 10), (11,), (12, 13), (14, 15), (16, 17), (18,), (19,), (20,))
    for turn in order:
        for g in running:
            for step in turn:
                next(g, None)
        for step in turn:
            for task in tasks.get(step, ()):
                task()


def write_out(*refs):
    for k in range(3):
        refs[3 + k][...] = refs[k][...]


def shards(
    leaf_rhs,
    mid_rhs,
    top_rhs,
    leaf_inverse,
    mid_inverse,
    top_inverse,
    leaf_coupling,
    mid_coupling,
    leaf_targets,
    leaf_counts,
    mid_targets,
    mid_counts,
):
    shape = leaf_rhs.shape
    rhs = shape[-1]
    n = rhs // CHAINS
    h = CHAINS
    vmem = pl.BlockSpec(memory_space=pltpu.VMEM)
    smem = pl.BlockSpec(memory_space=pltpu.SMEM)
    hbm = pl.BlockSpec(memory_space=pl.ANY)
    out = jax.ShapeDtypeStruct((TILE, rhs), F32)
    dma = pltpu.SemaphoreType.DMA
    weights = [pltpu.VMEM((2, k, GROUP, GROUP), BF) for k in (1, 2, 4, 2, 4, 4)]
    vectors = [pltpu.VMEM((h, 2, k, GROUP, n), BF) for k in (1, 4, 2, 4, 4)]
    outs = pl.pallas_call(
        functools.partial(kernel, n),
        out_shape=(out, out, out),
        in_specs=[vmem] * 3 + [hbm] * 5 + [smem] * 4,
        out_specs=(vmem, vmem, vmem),
        scratch_shapes=[
            pltpu.VMEM((GROUP, 8, TILE), BF),
            pltpu.VMEM((6, TILE, 8, TILE), BF),
            pltpu.VMEM((6, TILE, 8, TILE), BF),
            pltpu.VMEM((4, TILE, 16, TILE), BF),
            pltpu.VMEM((4, TILE, 16, TILE), BF),
            pltpu.VMEM((GROUP, 32, TILE), BF),
            *weights,
            *vectors,
            pltpu.VMEM((h, 4, TILE, n), F32),
            pltpu.VMEM((5, h, 4, TILE, n), BF),
            pltpu.VMEM((5, h, 3, TILE, n), BF),
            pltpu.VMEM((h, GROUP, n), F32),
            pltpu.VMEM((5, h, 4, n, TILE), BF),
            pltpu.VMEM((2, h, 4, n, GROUP), BF),
            pltpu.VMEM((2, h, 16, n, TILE), BF),
            pltpu.VMEM((3, h, 4, n, GROUP), BF),
            pltpu.VMEM((2, h, 2, n, GROUP), BF),
            pltpu.VMEM((1, h, 1, n, GROUP), BF),
            pltpu.VMEM((h, 16, n, TILE), BF),
            pltpu.VMEM((h, 16, n, TILE), BF),
            pltpu.VMEM((h, 8, n, TILE), BF),
            pltpu.VMEM((h, 16, n, TILE), BF),
            pltpu.VMEM((h, 4, n, TILE), BF),
            pltpu.VMEM((h, 4, n, TILE), F32),
            pltpu.VMEM((h, 2, 2, n, GROUP), F32),
            pltpu.VMEM((h, n, TILE), F32),
            pltpu.VMEM((h, n, TILE), F32),
            dma((9,)),
            dma((5, h, 4)),
            dma((5, h, 4)),
            dma((5, h, 4)),
            dma((5, h, 4)),
            dma((10, h)),
            dma((10, h)),
            dma((6, h)),
            dma((6, h, 4)),
            dma((6, h, 4)),
            dma((6, h, 4)),
        ],
        compiler_params=pltpu.CompilerParams(
            collective_id=0, has_side_effects=True, vmem_limit_bytes=62 * 2**20
        ),
        cost_estimate=pl.CostEstimate(flops=9_200_000_000, bytes_accessed=19_000_000, transcendentals=0),
    )(
        leaf_rhs.reshape(TILE, rhs),
        mid_rhs.reshape(TILE, rhs),
        top_rhs.reshape(TILE, rhs),
        leaf_inverse.reshape(GROUP, 8, TILE),
        mid_inverse.reshape(4, TILE, 16, TILE),
        top_inverse.reshape(GROUP, 32, TILE),
        leaf_coupling.reshape(4, 6, TILE, 8, TILE),
        mid_coupling.reshape(2, 4, TILE, 16, TILE),
        leaf_targets[0, 0],
        leaf_counts[0, 0],
        mid_targets[0, 0],
        mid_counts[0, 0],
    )
    outs = pl.pallas_call(
        write_out,
        out_shape=(out, out, out),
        in_specs=[vmem] * 3,
        out_specs=(vmem, vmem, vmem),
    )(*outs)
    return tuple(o.reshape(shape) for o in outs)


def solution(mesh):
    vector = P("leaf", "row", "col", None, None, None)
    inverse = P("leaf", "row", None, None, "col", None, None)
    coupling = P("leaf", "row", None, None, None, "col", None, None)
    placed = (
        vector,
        vector,
        vector,
        inverse,
        inverse,
        inverse,
        coupling,
        coupling,
        P("leaf", "row", None, None),
        P("leaf", "row", None),
        P("leaf", "row", None, None),
        P("leaf", "row", None),
    )
    return jax.shard_map(
        shards, mesh=mesh, in_specs=placed, out_specs=(vector, vector, vector), check_vma=False
    )
```

```python
import functools

import jax
import jax.numpy as jnp
from jax import lax
from jax.experimental import pallas as pl
from jax.experimental.pallas import tpu as pltpu
from jax.sharding import PartitionSpec as P

MESH = pl.DeviceIdType.MESH
TILE = 128
GROUP = 4 * TILE
CHAINS = 2
BF = jnp.bfloat16
F32 = jnp.float32


def kernel(
    width,
    leaf_rhs,
    mid_rhs,
    top_rhs,
    leaf_inv,
    mid_inv,
    top_inv,
    leaf_cpl,
    mid_cpl,
    leaf_tgt,
    leaf_cnt,
    mid_tgt,
    mid_cnt,
    leaf_out,
    mid_out,
    top_out,
    st_li,
    st_lc0,
    st_lc1,
    st_16a,
    st_16b,
    st_ti,
    wl,
    wm,
    wt,
    gm,
    gt,
    hm,
    x1,
    x2,
    x3,
    x4,
    x5,
    pf,
    xs,
    xr,
    top_part,
    yt,
    sib_s,
    pl_s,
    sib_r0,
    sib_r1,
    sib_r2,
    pl_r0,
    pl_r1,
    pl_r3,
    pl_r4,
    pl_r5,
    own,
    top_acc,
    lf,
    mf,
    w_sem,
    ag_rx,
    ag_rxs,
    ag_tx,
    ag_txs,
    x_rx,
    x_tx,
    rs_rx,
    rs_rxs,
    rs_tx,
    rs_txs,
):
    y = lax.axis_index("leaf")
    row = lax.axis_index("row")
    c = lax.axis_index("col")
    z, e = lax.div(row, 2), lax.rem(row, 2)
    eo = 1 - e
    half = lax.div(y, 2)
    par = lax.rem(y, 2)

    def partners(a):
        near = a + 1 - 2 * lax.rem(a, 2)
        return [a, near, lax.rem(a + 2, 4), lax.rem(near + 2, 4)]

    ys, zs, cs = partners(y), partners(z), partners(c)
    pars = [par, 1 - par]
    hops = (0, 1, 2, 1)
    sibling = (y, z * 2 + eo, c)

    def plane(dy, dz):
        return (ys[dy], zs[dz] * 2 + e, c)

    srcs = [2 * half, 2 * half + 1, 2 * (1 - half), 2 * (1 - half) + 1]
    fetch = {
        "li": pltpu.make_async_copy(leaf_inv, st_li, w_sem.at[0]),
        "lc0": pltpu.make_async_copy(leaf_cpl.at[srcs[0]], st_lc0, w_sem.at[1]),
        "lc1": pltpu.make_async_copy(leaf_cpl.at[srcs[1]], st_lc1, w_sem.at[2]),
        "mi": pltpu.make_async_copy(mid_inv, st_16a, w_sem.at[3]),
        "lc2": pltpu.make_async_copy(leaf_cpl.at[srcs[2]], st_lc0, w_sem.at[4]),
        "lc3": pltpu.make_async_copy(leaf_cpl.at[srcs[3]], st_lc1, w_sem.at[5]),
        "hm0": pltpu.make_async_copy(mid_cpl.at[0], st_16b, w_sem.at[6]),
        "hm1": pltpu.make_async_copy(mid_cpl.at[1], st_16a, w_sem.at[7]),
        "ti": pltpu.make_async_copy(top_inv, st_ti, w_sem.at[8]),
    }
    for name in ("li", "lc0", "lc1", "mi", "hm0", "ti"):
        fetch[name].start()

    def by_core(x, first, core):
        at = [(first + 2 * k + core) * TILE for k in range(4)]
        return jnp.concatenate([x[:, a : a + TILE] for a in at], axis=1)

    def lay_inverse(name, stage, dst, groups):
        fetch[name].wait()
        for q in range(4):
            rows = slice(q * TILE, (q + 1) * TILE)
            x = stage[rows].reshape(TILE, groups * 8 * TILE)
            for g in range(groups):
                for core in range(2):
                    dst[core, g, rows, :] = by_core(x, g * 8, core)

    def find_slot(targets, counts, k, v, slots):
        at, live = jnp.int32(0), jnp.int32(0)
        for m in range(slots):
            hit = jnp.logical_and(targets[k, m] == v, m < counts[k])
            at = jnp.where(hit, m, at)
            live = jnp.where(hit, 1, live)
        return at, live

    def lay_slot(x, live, width_tiles):
        x = x.reshape(TILE, width_tiles * TILE)
        return x * jnp.full(x.shape, live.astype(F32), F32).astype(BF)

    def lay_leaf_coupling(j):
        k = srcs[j]
        fetch[f"lc{j}"].wait()
        for v in range(0 if j < 2 else 4, 8):
            at, live = find_slot(leaf_tgt, leaf_cnt, k, v, 6)
            x = lay_slot((st_lc0, st_lc1)[j % 2][at], live, 8)
            rows = slice(v % 4 * TILE, (v % 4 + 1) * TILE)
            for core in range(2):
                if v < 4:
                    gm[core, j, rows, :] = by_core(x, 0, core)
                else:
                    gt[core, k, rows, :] = by_core(x, 0, core)
        if j < 2:
            fetch[f"lc{j + 2}"].start()

    def lay_mid_inverse():
        fetch["mi"].wait()
        for q in range(4):
            rows = slice(q * TILE, (q + 1) * TILE)
            x = st_16a[q].reshape(TILE, 16 * TILE)
            for g in range(2):
                for core in range(2):
                    wm[core, g, rows, :] = by_core(x, g * 8, core)
        fetch["hm1"].start()

    def lay_mid_coupling(k):
        fetch[f"hm{k}"].wait()
        for v in range(4):
            at, live = find_slot(mid_tgt, mid_cnt, k, v, 4)
            x = lay_slot((st_16b, st_16a)[k][at], live, 16)
            rows = slice(v * TILE, (v + 1) * TILE)
            for g in range(2):
                for core in range(2):
                    hm[core, 2 * k + g, rows, :] = by_core(x, g * 8, core)

    tasks = {
        0: [lambda: lay_inverse("li", st_li, wl, 1)],
        1: [lambda: lay_leaf_coupling(0), lambda: lay_leaf_coupling(1)],
        2: [lay_mid_inverse, lambda: lay_leaf_coupling(2)],
        3: [lambda: lay_leaf_coupling(3), lambda: lay_mid_coupling(0)],
        4: [lambda: lay_mid_coupling(1)],
        5: [lambda: lay_inverse("ti", st_ti, wt, 4)],
    }

    barrier = pltpu.get_barrier_semaphore()
    reached = [sibling] + [plane(0, k) for k in range(1, 4)] + [plane(k, 0) for k in range(1, 4)]
    reached += [(y, row, cs[k]) for k in range(1, 4)]
    for device in reached:
        pl.semaphore_signal(barrier, inc=1, device_id=device, device_id_type=MESH)
    pl.semaphore_wait(barrier, len(reached))

    def remote(src, dst, tx, rx, device):
        return pltpu.make_async_remote_copy(
            src_ref=src, dst_ref=dst, send_sem=tx, recv_sem=rx, device_id=device, device_id_type=MESH
        )

    def chain(h):
        sent = []
        cols = slice(h * width, (h + 1) * width)

        def drain():
            for ref, sem in sent:
                remote(ref, ref, sem, sem, sibling).wait_send()
            sent.clear()

        def arrived(ref, sem):
            remote(ref, ref, sem, sem, sibling).wait_recv()

        def gather_send(ph, x, at, value, dys, later=()):
            mine = x.at[h, e, at[0], pl.ds(z * TILE, TILE)]
            x[h, e, at[0], pl.ds(z * TILE, TILE), :] = value
            far_first = sorted(
                ((dy, dz) for dy in dys for dz in range(4) if dy or dz), key=lambda p: -hops[p[0]] - hops[p[1]]
            )
            far_first += [(dy, dz) for dy in later for dz in (2, 1, 3, 0)]
            for dy, dz in far_first:
                remote(mine, mine, ag_tx.at[ph, h, dy], ag_rx.at[ph, h, dy], plane(dy, dz)).start()
            for dy in (*dys, *later):
                tiles = 4 if dy else 3
                sent.append((x.at[h, 0, 0, pl.ds(0, tiles * TILE)], ag_tx.at[ph, h, dy]))

        def gather_forward(ph, x, at, dy):
            tiles = 4 if dy else 3
            arrived(x.at[h, e, at[dy], pl.ds(0, tiles * TILE)], ag_rx.at[ph, h, dy])
            block = x.at[h, e, at[dy]]
            remote(block, block, ag_txs.at[ph, h, dy], ag_rxs.at[ph, h, dy], sibling).start()
            sent.append((block, ag_txs.at[ph, h, dy]))

        def gather_done(ph, x, at, dy):
            arrived(x.at[h, eo, at[dy]], ag_rxs.at[ph, h, dy])

        def gathered_product(ph, w, wat, x, at, dys):
            def part(core, dy):
                return jnp.dot(w[core, wat[dy]], x[h, core, at[dy]], preferred_element_type=F32)

            total = None
            for k, dy in enumerate(dys):
                if k == 1:
                    yield
                gather_forward(ph, x, at, dy)
                total = part(e, dy) if total is None else total + part(e, dy)
            if len(dys) == 1:
                yield
            for dy in dys:
                gather_done(ph, x, at, dy)
                total = total + part(eo, dy)
            return total

        def column_send(ph, total):
            for q in range(4):
                tile = total[q * TILE : (q + 1) * TILE]
                pf[h, q] = tile
                xs[ph, h, q] = tile.astype(BF)
            for dc in (2, 1, 3):
                remote(
                    xs.at[ph, h, cs[dc]], xr.at[ph, h, dc - 1], x_tx.at[ph, h], x_rx.at[ph, h], (y, row, cs[dc])
                ).start()
            sent.append((xs.at[ph, h, pl.ds(0, 3)], x_tx.at[ph, h]))

        def column_sum(ph):
            arrived(xr.at[ph, h], x_rx.at[ph, h])
            total = pf[h, c]
            for k in range(3):
                total = total + xr[ph, h, k].astype(F32)
            return total

        def row_send(ph, value):
            mine = yt.at[ph, h, c]
            yt[ph, h, c] = value
            for dc in (2, 1, 3):
                remote(mine, mine, x_tx.at[5 + ph, h], x_rx.at[5 + ph, h], (y, row, cs[dc])).start()
            sent.append((yt.at[ph, h, pl.ds(0, 3)], x_tx.at[5 + ph, h]))

        def row_tiles(ph):
            arrived(yt.at[ph, h, pl.ds(0, 3)], x_rx.at[5 + ph, h])
            return jnp.concatenate([yt[ph, h, q] for q in range(4)], axis=1)

        def group_send(ph, piece, s_at, sib_r, r_at, pl_r, dys):
            for k, dy in enumerate(dys):
                sib_s[s_at, h, dy] = piece(0, dy).astype(BF)
                remote(
                    sib_s.at[s_at, h, dy], sib_r.at[r_at, h, dy], rs_txs.at[ph, h, dy], rs_rxs.at[ph, h, dy], sibling
                ).start()
                sent.append((sib_s.at[s_at, h, dy], rs_txs.at[ph, h, dy]))
            for dy in dys:
                total = piece(1, dy)
                arrived(sib_r.at[r_at, h, dy], rs_rxs.at[ph, h, dy])
                total = total + sib_r[r_at, h, dy].astype(F32)
                for k in range(4):
                    tile = total[:, k * TILE : (k + 1) * TILE]
                    pl_s[s_at, h, dy * 4 + k] = tile.astype(BF)
                    if dy == 0:
                        own[h, k] = tile
                for dz in (2, 1, 3, 0):
                    if dy or dz:
                        remote(
                            pl_s.at[s_at, h, dy * 4 + zs[dz]],
                            pl_r.at[h, dy * 4 + dz],
                            rs_tx.at[ph, h, dy],
                            rs_rx.at[ph, h],
                            plane(dy, dz),
                        ).start()
                tiles = 4 if dy else 3
                sent.append((pl_s.at[s_at, h, pl.ds(0, tiles)], rs_tx.at[ph, h, dy]))

        def group_sum(ph, pl_r, tiles):
            arrived(pl_r.at[h, pl.ds(1, tiles)], rs_rx.at[ph, h])
            total = own[h, z]
            for k in range(1, tiles + 1):
                total = total + pl_r[h, k].astype(F32)
            return total

        zero = [0]
        far = (2, 1, 3, 0)

        gather_send(0, x1, zero, leaf_rhs[:, cols].astype(BF), (0,))
        yield
        total = yield from gathered_product(0, wl, zero, x1, zero, (0,))
        column_send(0, total)
        yield
        drain()
        forward = column_sum(0)
        gather_send(1, x2, ys, forward.astype(BF), (1, 0), (2, 3))
        lf[h] = forward.T
        yield
        total = yield from gathered_product(1, gm, pars, x2, ys, (0, 1))
        column_send(1, total)
        yield
        drain()
        gather_send(2, x3, pars, (mid_rhs[:, cols] - column_sum(1)).astype(BF), (1, 0))
        for dy in (3, 2):
            gather_forward(1, x2, ys, dy)
        yield
        total = yield from gathered_product(2, wm, pars, x3, pars, (0, 1))
        column_send(2, total)
        for dy in (3, 2):
            gather_done(1, x2, ys, dy)
        total = None
        for core in (e, eo):
            for dy in far:
                part = jnp.dot(gt[core, ys[dy]], x2[h, core, ys[dy]], preferred_element_type=F32)
                total = part if total is None else total + part
        top_part[h] = total
        yield
        drain()
        forward = column_sum(2)
        gather_send(3, x4, ys, forward.astype(BF), far)
        mf[h] = forward.T
        yield
        total = yield from gathered_product(3, hm, ys, x4, ys, (0, 1, 3, 2))
        column_send(3, total + top_part[h])
        yield
        drain()
        gather_send(4, x5, ys, (top_rhs[:, cols] - column_sum(3)).astype(BF), far)
        yield
        total = yield from gathered_product(4, wt, ys, x5, ys, (0, 1, 3, 2))
        column_send(4, total)
        yield
        drain()
        row_send(0, column_sum(4).T.astype(BF))
        yield

        def both(w, wat, values):
            def piece(mine, dy):
                return jnp.dot(values, w[e if mine else eo, wat[dy]], preferred_element_type=F32)

            return piece

        values = row_tiles(0)
        group_send(0, both(wt, ys, values), 0, sib_r0, 0, pl_r0, far)
        yield
        drain()
        solution_t = group_sum(0, pl_r0, 15)
        row_send(1, solution_t.astype(BF))
        top_out[:, cols] = solution_t.T
        yield
        values = row_tiles(1)
        group_send(1, both(hm, ys, values), 1, sib_r0, 1, pl_r1, far)
        part = both(gt, ys, values)
        for mine in range(2):
            for dy in range(2):
                top_acc[h, mine, dy] = part(mine, dy)
        yield
        drain()
        row_send(2, (mf[h] - group_sum(1, pl_r1, 15)).astype(BF))
        group_send(2, part, 0, sib_r0, 2, pl_r4, (2, 3))
        yield
        values = row_tiles(2)
        group_send(3, both(wm, pars, values), 1, sib_r1, 0, pl_r3, (1, 0))
        yield
        drain()
        solution_t = group_sum(3, pl_r3, 7)
        row_send(3, solution_t.astype(BF))
        mid_out[:, cols] = solution_t.T
        arrived(pl_r4.at[h, pl.ds(8, 8)], rs_rx.at[2, h])
        late = lf[h]
        for k in range(8, 16):
            late = late - pl_r4[h, k].astype(F32)
        lf[h] = late
        yield
        values = row_tiles(3)
        mid_piece = both(gm, pars, values)
        group_send(
            4, lambda mine, dy: mid_piece(mine, dy) + top_acc[h, mine, dy], 0, sib_r1, 1, pl_r4, (1, 0)
        )
        yield
        drain()
        row_send(4, (lf[h] - group_sum(4, pl_r4, 7)).astype(BF))
        yield
        values = row_tiles(4)
        group_send(5, both(wl, zero, values), 1, sib_r2, 0, pl_r5, (0,))
        yield
        drain()
        leaf_out[:, cols] = group_sum(5, pl_r5, 3).T
        drain()

    running = [chain(h) for h in range(CHAINS)]
    for what in "ab0aaba1bab2aba3bab4aba5babababababababbaabbaabbaabbababab":
        if what.isdigit():
            for task in tasks[int(what)]:
                task()
        else:
            next(running["ab".index(what)], None)


def write_out(*refs):
    for k in range(3):
        refs[3 + k][...] = refs[k][...]


def shards(
    leaf_rhs,
    mid_rhs,
    top_rhs,
    leaf_inverse,
    mid_inverse,
    top_inverse,
    leaf_coupling,
    mid_coupling,
    leaf_targets,
    leaf_counts,
    mid_targets,
    mid_counts,
):
    shape = leaf_rhs.shape
    rhs = shape[-1]
    n = rhs // CHAINS
    h = CHAINS
    vmem = pl.BlockSpec(memory_space=pltpu.VMEM)
    smem = pl.BlockSpec(memory_space=pltpu.SMEM)
    hbm = pl.BlockSpec(memory_space=pl.ANY)
    out = jax.ShapeDtypeStruct((TILE, rhs), F32)
    dma = pltpu.SemaphoreType.DMA
    weights = [pltpu.VMEM((2, k, GROUP, GROUP), BF) for k in (1, 2, 4, 2, 4, 4)]
    vectors = [pltpu.VMEM((h, 2, k, GROUP, n), BF) for k in (1, 4, 2, 4, 4)]
    outs = pl.pallas_call(
        functools.partial(kernel, n),
        out_shape=(out, out, out),
        in_specs=[vmem] * 3 + [hbm] * 5 + [smem] * 4,
        out_specs=(vmem, vmem, vmem),
        scratch_shapes=[
            pltpu.VMEM((GROUP, 8, TILE), BF),
            pltpu.VMEM((6, TILE, 8, TILE), BF),
            pltpu.VMEM((6, TILE, 8, TILE), BF),
            pltpu.VMEM((4, TILE, 16, TILE), BF),
            pltpu.VMEM((4, TILE, 16, TILE), BF),
            pltpu.VMEM((GROUP, 32, TILE), BF),
            *weights,
            *vectors,
            pltpu.VMEM((h, 4, TILE, n), F32),
            pltpu.VMEM((5, h, 4, TILE, n), BF),
            pltpu.VMEM((5, h, 3, TILE, n), BF),
            pltpu.VMEM((h, GROUP, n), F32),
            pltpu.VMEM((5, h, 4, n, TILE), BF),
            pltpu.VMEM((2, h, 4, n, GROUP), BF),
            pltpu.VMEM((2, h, 16, n, TILE), BF),
            pltpu.VMEM((3, h, 4, n, GROUP), BF),
            pltpu.VMEM((2, h, 2, n, GROUP), BF),
            pltpu.VMEM((1, h, 1, n, GROUP), BF),
            pltpu.VMEM((h, 16, n, TILE), BF),
            pltpu.VMEM((h, 16, n, TILE), BF),
            pltpu.VMEM((h, 8, n, TILE), BF),
            pltpu.VMEM((h, 16, n, TILE), BF),
            pltpu.VMEM((h, 4, n, TILE), BF),
            pltpu.VMEM((h, 4, n, TILE), F32),
            pltpu.VMEM((h, 2, 2, n, GROUP), F32),
            pltpu.VMEM((h, n, TILE), F32),
            pltpu.VMEM((h, n, TILE), F32),
            dma((9,)),
            dma((5, h, 4)),
            dma((5, h, 4)),
            dma((5, h, 4)),
            dma((5, h, 4)),
            dma((10, h)),
            dma((10, h)),
            dma((6, h)),
            dma((6, h, 4)),
            dma((6, h, 4)),
            dma((6, h, 4)),
        ],
        compiler_params=pltpu.CompilerParams(
            collective_id=0, has_side_effects=True, vmem_limit_bytes=62 * 2**20
        ),
        cost_estimate=pl.CostEstimate(flops=9_200_000_000, bytes_accessed=19_000_000, transcendentals=0),
    )(
        leaf_rhs.reshape(TILE, rhs),
        mid_rhs.reshape(TILE, rhs),
        top_rhs.reshape(TILE, rhs),
        leaf_inverse.reshape(GROUP, 8, TILE),
        mid_inverse.reshape(4, TILE, 16, TILE),
        top_inverse.reshape(GROUP, 32, TILE),
        leaf_coupling.reshape(4, 6, TILE, 8, TILE),
        mid_coupling.reshape(2, 4, TILE, 16, TILE),
        leaf_targets[0, 0],
        leaf_counts[0, 0],
        mid_targets[0, 0],
        mid_counts[0, 0],
    )
    outs = pl.pallas_call(
        write_out,
        out_shape=(out, out, out),
        in_specs=[vmem] * 3,
        out_specs=(vmem, vmem, vmem),
    )(*outs)
    return tuple(o.reshape(shape) for o in outs)


def solution(mesh):
    vector = P("leaf", "row", "col", None, None, None)
    inverse = P("leaf", "row", None, None, "col", None, None)
    coupling = P("leaf", "row", None, None, None, "col", None, None)
    placed = (
        vector,
        vector,
        vector,
        inverse,
        inverse,
        inverse,
        coupling,
        coupling,
        P("leaf", "row", None, None),
        P("leaf", "row", None),
        P("leaf", "row", None, None),
        P("leaf", "row", None),
    )
    return jax.shard_map(
        shards, mesh=mesh, in_specs=placed, out_specs=(vector, vector, vector), check_vma=False
    )
```
